1024 devices in a mesh: blk: 256 (over x, y_lo, z, core), grp: 4 (over y_hi).
Axes of the slice: x: 8, y: 8 (y_hi: 4, y_lo: 2; y = y_hi * 2 + y_lo), z: 8, core: 2. Of those that a mesh axis runs over, the one named last changes fastest.
Arguments:
- images: bfloat16 [131072, 1152], P(('blk', 'grp')), may hold values from -6 to 6
- texts: bfloat16 [131072, 1152], P(('blk', 'grp')), may hold values from -6 to 6
- scale: float32 [1], replicated, may hold values from 0.02 to 0.08
- bias: float32 [1], replicated, may hold values from -4 to -1
Outputs:
- loss_rows: float32 [131072], P(('blk', 'grp'))
- grad_images: float32 [131072, 1152], P(('blk', 'grp'))
- grad_texts: float32 [131072, 1152], P(('blk', 'grp'))
The draws below stay inside these ranges and needn't reach their ends.
All inputs are finite; a program needn't handle non-finite values.
Results may differ from the reference program's by a relative error of at most 0.0023.
Values may be sent and summed in bfloat16 or wider, within the bound.
A program may use at most 32 MiB of HBM per device.

```python
import math
import jax
import jax.numpy as jnp

D = 1152
ROWS_DEV = 128
STEPS = 8
TOKENS = 131072
N_BLK = 256
N_GRP = 4


def shard_levels(key, shape, pieces, least, top_value):
    factor_of, own = 1.0, jax.random.fold_in(key, 6)
    for dim, parts in pieces:
        steps = jnp.exp(jax.random.uniform(jax.random.fold_in(own, dim), (parts,), jnp.float32, least / len(pieces), top_value / len(pieces)))
        factor_of = factor_of * jnp.repeat(steps, shape[dim] // parts).reshape([-1 if axis == dim else 1 for axis in range(len(shape))])
    return factor_of


def noise(rng, extent, deviation, reach, pieces=(), held_as=jnp.bfloat16):
    array = jax.random.normal(rng, extent, jnp.float32) * deviation
    if len(pieces) > 0:
        array = shard_levels(rng, extent, pieces, -0.22, 0.18) * array
    return jnp.clip(array, min=-reach, max=reach).astype(held_as)


def setup_inputs(seed: int = 0) -> dict:
    keys = jax.random.split(jax.random.key(seed), 5)
    images = noise(keys[0], (TOKENS, D), 1.0, 6.0, ((0, 1024),))
    texts = noise(keys[1], (TOKENS, D), 1.0, 6.0, ((0, 1024),))
    scale = jnp.clip(jnp.exp(jax.random.uniform(keys[2], (1,), jnp.float32, math.log(0.02), math.log(0.08))), 0.02, 0.08)
    bias = jnp.clip(jax.random.uniform(keys[3], (1,), jnp.float32, -4.0, -1.0), -4.0, -1.0)
    return {"images": images, "texts": texts, "scale": scale, "bias": bias}


def pair_block(image_blocks, partner, scale, bias, positive):
    logits = scale[0] * jnp.einsum("bgid,bgjd->bgij", image_blocks.astype(jnp.float32), partner.astype(jnp.float32)) + bias[0]
    rows = image_blocks.shape[2]
    diagonal = jnp.arange(rows)[:, None] == jnp.arange(rows)[None, :]
    if positive:
        sign = jnp.where(diagonal, 1.0, -1.0).astype(jnp.float32)
    else:
        sign = -jnp.ones((rows, rows), jnp.float32)
    loss = jnp.sum(-jax.nn.log_sigmoid(sign * logits), axis=3)
    coef = (-sign * jax.nn.sigmoid(-sign * logits)).astype(jnp.bfloat16).astype(jnp.float32)
    grad_img = jnp.einsum("bgij,bgjd->bgid", coef, partner.astype(jnp.float32))
    grad_txt = jnp.einsum("bgij,bgid->bgjd", coef, image_blocks.astype(jnp.float32))
    return loss, grad_img, grad_txt


def reference(images, texts, scale, bias):
    image_blocks = images.reshape(N_BLK, N_GRP, ROWS_DEV, D)
    text_blocks = texts.reshape(N_BLK, N_GRP, ROWS_DEV, D)
    loss_total = jnp.zeros((N_BLK, N_GRP, ROWS_DEV), jnp.float32)
    grad_img = jnp.zeros((N_BLK, N_GRP, ROWS_DEV, D), jnp.float32)
    grad_txt = jnp.zeros((N_BLK, N_GRP, ROWS_DEV, D), jnp.float32)
    for step in range(STEPS):
        partner = jnp.roll(text_blocks, step, axis=0)
        loss, g_img, g_txt = pair_block(image_blocks, partner, scale, bias, step == 0)
        loss_total = loss_total + loss
        grad_img = grad_img + g_img
        grad_txt = grad_txt + jnp.roll(g_txt, -step, axis=0)
    partner = jnp.roll(text_blocks, 1, axis=1)
    loss, g_img, g_txt = pair_block(image_blocks, partner, scale, bias, False)
    loss_total = loss_total + loss
    grad_img = grad_img + g_img
    grad_txt = grad_txt + jnp.roll(g_txt, -1, axis=1)
    return (loss_total.reshape(TOKENS), (scale[0] * grad_img).reshape(TOKENS, D), (scale[0] * grad_txt).reshape(TOKENS, D))
```

```python
import functools

import jax
import jax.numpy as jnp
from jax import lax
from jax.experimental import pallas as pl
from jax.experimental.pallas import tpu as pltpu
from jax.sharding import PartitionSpec as P

HOPS = 3
CHUNKS = 2
VMEM_LIMIT = 48 * 2**20
MESH = pl.DeviceIdType.MESH


def kernel(
    n_blk,
    n_grp,
    images,
    texts,
    scale_in,
    bias_in,
    loss_out,
    grad_out,
    own,
    pair,
    ext,
    cross,
    acc,
    lacc,
    load_sem,
    send_sem,
    hop_send,
    hop_sem,
    sib_sem,
    ext_sem,
    cross_sem,
    ready_sem,
    scale,
    bias,
):
    rows = own.shape[1]
    piece = rows // CHUNKS
    b = lax.axis_index("blk")
    g = lax.axis_index("grp")
    c = lax.rem(b, 2)
    z = lax.rem(b // 2, 8)

    def at(db, dg=0):
        return (lax.rem(b + db + n_blk, n_blk), lax.rem(g + dg + n_grp, n_grp))

    sib = at(1 - 2 * c)
    along = (at(2), at(-2))
    along2 = (at(4), at(-4))
    nextdoor = (at(1), at(-1))
    over = (at(0, 1), at(0, -1))
    source = (texts, images)

    loads = [
        pltpu.make_async_copy(images, own.at[0], load_sem.at[0]),
        pltpu.make_async_copy(texts, own.at[1], load_sem.at[1]),
        pltpu.make_async_copy(scale_in, scale, load_sem.at[2]),
        pltpu.make_async_copy(bias_in, bias, load_sem.at[3]),
    ]
    for load in loads:
        load.start()

    first, last = z == 0, z == 7
    inner_up, inner_down = z != 7, z != 0
    greets = (
        (along[0], inner_up),
        (along[1], first),
        (nextdoor[0], jnp.logical_or(c == 0, inner_up)),
        (nextdoor[1], jnp.logical_and(c == 0, first)),
        (over[0], g < 2),
        (over[1], jnp.logical_or(g == 0, g == 3)),
    )
    greeted = (
        (along[0], last),
        (along[1], inner_down),
        (nextdoor[0], jnp.logical_and(c == 1, last)),
        (nextdoor[1], jnp.logical_or(c == 1, inner_down)),
        (over[0], jnp.logical_or(g == 2, g == 3)),
        (over[1], jnp.logical_or(g == 1, g == 2)),
    )
    mirror = (1, 0, 3, 2, 5, 4)
    barrier = pltpu.get_barrier_semaphore()
    for device, when in greets:

        @pl.when(when)
        def _():
            pl.semaphore_signal(barrier, inc=1, device_id=device, device_id_type=MESH)

    here_first = sum(jnp.where(when, 1, 0) for _, when in greeted)

    @pl.when(here_first > 0)
    def _():
        pl.semaphore_wait(barrier, here_first)

    for n, (device, when) in enumerate(greeted):

        @pl.when(when)
        def _():
            pl.semaphore_signal(
                ready_sem.at[mirror[n]], inc=1, device_id=device, device_id_type=MESH
            )

    def ready(n, when):
        @pl.when(jnp.logical_and(greets[n][1], when))
        def _():
            pl.semaphore_wait(ready_sem.at[n], 1)

    sent = []

    def copy_to(src, dst, recv, device, sem):
        return pltpu.make_async_remote_copy(
            src_ref=src,
            dst_ref=dst,
            send_sem=sem,
            recv_sem=recv,
            device_id=device,
            device_id_type=MESH,
        )

    def send(src, dst, recv, device, when):
        copy = copy_to(src, dst, recv, device, send_sem.at[len(sent)])
        sent.append((copy, when))
        pl.when(when)(copy.start)

    def arrived(dst, recv):
        pltpu.make_async_remote_copy(
            src_ref=dst,
            dst_ref=dst,
            send_sem=send_sem.at[0],
            recv_sem=recv,
            device_id=sib,
            device_id_type=MESH,
        ).wait_recv()

    def part(k):
        return pl.ds(k * piece, piece)

    def lane(s, hop, k, core):
        start = pl.multiple_of(core * rows + k * piece, piece)
        return pair.at[s, hop, pl.ds(start, piece), :]

    def send_own(s, when):
        for k in range(CHUNKS):
            send(source[s].at[part(k)], lane(s, 0, k, c), hop_sem.at[s, 0, k], along[s], when)

    def send_cross(when):
        for s in range(2):
            send(source[s], cross.at[s], cross_sem.at[s], over[s], when)

    send_own(1, inner_down)
    send(images, ext.at[1], ext_sem.at[1], nextdoor[1], c == 1)
    ready(0, inner_up)
    send_own(0, g >= 0)
    ready(2, c == 0)
    send(texts, ext.at[0], ext_sem.at[0], nextdoor[0], c == 0)
    ready(4, g >= 0)
    ready(5, g >= 0)
    send_cross(inner_up)

    def meet(side, block, positive=False, first=False):
        values = block[...]
        dots = lax.dot_general(
            own[side], values, (((1,), (1,)), ((), ())), preferred_element_type=jnp.float32
        )
        score = factor * dots + offset
        if positive:
            diagonal = lax.broadcasted_iota(jnp.int32, score.shape, 0) == lax.broadcasted_iota(
                jnp.int32, score.shape, 1
            )
            score = jnp.where(diagonal, -score, score)
        small = jnp.exp(-jnp.abs(score))
        share = 1.0 / (1.0 + small)
        coef = jnp.where(score >= 0, share, small * share)
        if positive:
            coef = jnp.where(diagonal, -coef, coef)
        term = jnp.maximum(score, 0.0) + jnp.log1p(small)
        if score.shape[1] > rows:
            term = term[:, :rows] + term[:, rows:]
        grad = jnp.dot(coef.astype(jnp.bfloat16), values, preferred_element_type=jnp.float32)
        if first:
            lacc[side] = term
            acc[side] = grad
        else:
            lacc[side] += term
            acc[side] += grad

    for load in loads:
        load.wait()
    factor, offset = scale[0], bias[0]
    for side in range(2):
        meet(side, own.at[1 - side], positive=True, first=True)

    def meet_cross(when):
        @pl.when(when)
        def _():
            for s in range(2):
                arrived(cross.at[s], cross_sem.at[s])

            @pl.loop(0, 2)
            def _(s):
                meet(s, cross.at[s])

    ready(2, c == 1)
    meet_cross(first)
    ready(1, first)
    ready(3, first)
    send_own(1, first)

    code = jnp.where(first, 19, jnp.where(z == 1, 22, jnp.where(last, 50, 42)))

    def stream_hop(i):
        s = lax.rem(code // (1 << i), 2)
        ups = sum(lax.rem(code // (1 << j), 2) for j in range(i)) if i else 0
        return s, jnp.where(s == 1, ups, i - ups)

    steps = [stream_hop(i) for i in range(2 * HOPS)]

    def forwards(i, k):
        s, hop = steps[i]
        here = lane(s, hop, k, c)
        further = lane(s, lax.rem(hop + 1, HOPS), k, c)
        n = i * CHUNKS + k
        return (
            (
                copy_to(here, further, hop_sem.at[s, lax.rem(hop + 1, HOPS), k], at(2 - 4 * s), hop_send.at[n, 0]),
                hop + 1 < HOPS,
            ),
            (
                copy_to(here, ext.at[s, part(k)], late_sem(ext_sem, s, k), at(1 - 2 * s), hop_send.at[n, 0]),
                jnp.logical_and(hop + 1 == HOPS, c == 1 - s),
            ),
            (copy_to(here, here, sib_sem.at[s, hop, k], sib, hop_send.at[n, 1]), g >= 0),
        )

    for i in range(2 * HOPS + 1):
        if i < 2 * HOPS:
            s, hop = steps[i]
            for k in range(CHUNKS):
                arrived(lane(s, hop, k, c), hop_sem.at[s, hop, k])
                for copy, when in forwards(i, k):
                    pl.when(when)(copy.start)
        if i == 1:
            early = 1 - c
            arrived(ext.at[early], ext_sem.at[early])
            meet(early, ext.at[early])
        if i == 3:
            meet_cross(jnp.logical_and(inner_up, inner_down))
            send_cross(last)
        if i >= 1:
            s, hop = steps[i - 1]
            for k in range(CHUNKS):
                arrived(lane(s, hop, k, 1 - c), sib_sem.at[s, hop, k])
            meet(s, pair.at[s, hop])
    meet_cross(last)
    for k in range(CHUNKS):
        arrived(ext.at[c, part(k)], late_sem(ext_sem, c, k))
    meet(c, ext.at[c])

    for side in range(2):
        grad_out[side] = factor * acc[side]
    loss_out[...] = jnp.sum(lacc[0].T, axis=0, keepdims=True)
    for copy, when in sent:
        pl.when(when)(copy.wait_send)
    for i in range(2 * HOPS):
        for k in range(CHUNKS):
            for copy, when in forwards(i, k):
                pl.when(when)(copy.wait_send)


def late_sem(ext_sem, s, k):
    return ext_sem.at[2 + 2 * k + s]


def hand_over(loss_in, grad_in, loss_out, gimg_out, gtxt_out, sem):
    half = gimg_out.shape[0] // 2
    copies = [pltpu.make_async_copy(loss_in, loss_out, sem.at[4])]
    for side, out in enumerate((gimg_out, gtxt_out)):
        for k in range(2):
            rows = pl.ds(k * half, half)
            copies.append(
                pltpu.make_async_copy(grad_in.at[side, rows], out.at[rows], sem.at[2 * side + k])
            )
    for copy in copies:
        copy.start()
    for copy in copies:
        copy.wait()


def solution(mesh):
    n_blk, n_grp = mesh.shape["blk"], mesh.shape["grp"]

    def on_device(images, texts, scale, bias):
        rows, width = images.shape
        bf16, f32 = jnp.bfloat16, jnp.float32
        hbm = pl.BlockSpec(memory_space=pltpu.HBM)
        vmem = pl.BlockSpec(memory_space=pltpu.VMEM)
        anywhere = pl.BlockSpec(memory_space=pl.ANY)
        loss, grads = pl.pallas_call(
            functools.partial(kernel, n_blk, n_grp),
            out_shape=(
                jax.ShapeDtypeStruct((1, rows), f32),
                jax.ShapeDtypeStruct((2, rows, width), f32),
            ),
            in_specs=[hbm] * 4,
            out_specs=(vmem, vmem),
            scratch_shapes=[
                pltpu.VMEM((2, rows, width), bf16),
                pltpu.VMEM((2, HOPS, 2 * rows, width), bf16),
                pltpu.VMEM((2, rows, width), bf16),
                pltpu.VMEM((2, rows, width), bf16),
                pltpu.VMEM((2, rows, width), f32),
                pltpu.VMEM((2, rows, rows), f32),
                pltpu.SemaphoreType.DMA((4,)),
                pltpu.SemaphoreType.DMA((3 * CHUNKS + 6,)),
                pltpu.SemaphoreType.DMA((2 * HOPS * CHUNKS, 2)),
                pltpu.SemaphoreType.DMA((2, HOPS, CHUNKS)),
                pltpu.SemaphoreType.DMA((2, HOPS, CHUNKS)),
                pltpu.SemaphoreType.DMA((2 + 2 * CHUNKS,)),
                pltpu.SemaphoreType.DMA((2,)),
                pltpu.SemaphoreType.REGULAR((6,)),
                pltpu.SMEM((1,), f32),
                pltpu.SMEM((1,), f32),
            ],
            compiler_params=pltpu.CompilerParams(
                collective_id=0, has_side_effects=True, vmem_limit_bytes=VMEM_LIMIT
            ),
        )(images, texts, scale, bias)
        loss, gimg, gtxt = pl.pallas_call(
            hand_over,
            out_shape=(
                jax.ShapeDtypeStruct((1, rows), f32),
                jax.ShapeDtypeStruct((rows, width), f32),
                jax.ShapeDtypeStruct((rows, width), f32),
            ),
            in_specs=[anywhere] * 2,
            out_specs=(anywhere,) * 3,
            scratch_shapes=[pltpu.SemaphoreType.DMA((5,))],
            compiler_params=pltpu.CompilerParams(vmem_limit_bytes=VMEM_LIMIT),
        )(loss, grads)
        return loss.reshape(rows), gimg, gtxt

    block = P(("blk", "grp"), None)
    return jax.shard_map(
        on_device,
        mesh=mesh,
        in_specs=(block, block, P(), P()),
        out_specs=(P(("blk", "grp")), block, block),
        check_vma=False,
    )
```

```python
import functools

import jax
import jax.numpy as jnp
from jax import lax
from jax.experimental import pallas as pl
from jax.experimental.pallas import tpu as pltpu
from jax.sharding import PartitionSpec as P

HOPS = 3
CHUNKS = 4
RELAY_AT = 2
CROSS_AT = 0
VMEM_LIMIT = 48 * 2**20
MESH = pl.DeviceIdType.MESH


def kernel(
    n_blk,
    n_grp,
    images,
    texts,
    scale_in,
    bias_in,
    loss_out,
    grad_out,
    own,
    pair,
    ext,
    cross,
    acc,
    lacc,
    load_sem,
    relay,
    relay_sem,
    send_sem,
    hop_send,
    hop_sem,
    sib_sem,
    ext_sem,
    cross_sem,
    ready_sem,
    scale,
    bias,
):
    rows = own.shape[1]
    piece = rows // CHUNKS
    b = lax.axis_index("blk")
    g = lax.axis_index("grp")
    c = lax.rem(b, 2)
    z = lax.rem(b // 2, 8)

    def is_root(device):
        return jnp.logical_and(device[0] == 0, device[1] == 0)

    def at(db, dg=0):
        return (lax.rem(b + db + n_blk, n_blk), lax.rem(g + dg + n_grp, n_grp))

    sib = at(1 - 2 * c)
    along = (at(2), at(-2))
    along2 = (at(4), at(-4))
    nextdoor = (at(1), at(-1))
    over = (at(0, 1), at(0, -1))
    source = (texts, images)

    loads = [
        pltpu.make_async_copy(images, own.at[0], load_sem.at[0]),
        pltpu.make_async_copy(texts, own.at[1], load_sem.at[1]),
        pltpu.make_async_copy(scale_in, scale, load_sem.at[2]),
        pltpu.make_async_copy(bias_in, bias, load_sem.at[3]),
    ]
    for load in loads:
        load.start()

    first, last = z == 0, z == 7
    inner_up, inner_down = z != 7, z != 0
    greets = (
        (along[0], inner_up),
        (along[1], first),
        (nextdoor[0], jnp.logical_or(c == 0, inner_up)),
        (nextdoor[1], jnp.logical_and(c == 0, first)),
        (over[0], g < 2),
        (over[1], jnp.logical_or(g == 0, g == 3)),
    )
    greeted = (
        (along[0], last),
        (along[1], inner_down),
        (nextdoor[0], jnp.logical_and(c == 1, last)),
        (nextdoor[1], jnp.logical_or(c == 1, inner_down)),
        (over[0], jnp.logical_or(g == 2, g == 3)),
        (over[1], jnp.logical_or(g == 1, g == 2)),
    )
    mirror = (1, 0, 3, 2, 5, 4)
    root = is_root((b, g))
    def flips(n, to):
        near_root = jnp.logical_and(is_root(to), z != 7)
        return near_root if n in (1, 3) else jnp.logical_or(root, near_root)

    greets = tuple(
        (to, jnp.where(flips(n, to), ~root, when)) for n, (to, when) in enumerate(greets)
    )
    greeted = tuple(
        (to, jnp.where(flips(n, to), root, when)) for n, (to, when) in enumerate(greeted)
    )
    far_to_root = jnp.logical_and(z == 3, jnp.where(c == 0, is_root(at(10)), is_root(at(9))))
    even, odd = c == 0, c == 1
    far_greets = (
        (at(-4), first),
        (at(-6), jnp.logical_and(first, odd)),
        (at(-9), jnp.logical_and(first, jnp.logical_and(even, ~root))),
        (at(-10), jnp.logical_and(first, jnp.logical_and(even, ~root))),
        ((0, 0), far_to_root),
        (at(-9), jnp.logical_and(z == 4, even)),
        (at(4), jnp.logical_and(z == 3, even)),
    )
    end = jnp.logical_and(last, odd)
    far_greeted = jnp.where(
        jnp.logical_or(jnp.logical_or(z == 3, end), jnp.logical_or(z == 5, z == 6)), 1, 0
    )
    far_greeted = jnp.where(far_to_root, 0, jnp.where(root, 2, far_greeted))
    barrier = pltpu.get_barrier_semaphore()
    for device, when in greets + far_greets:

        @pl.when(when)
        def _():
            pl.semaphore_signal(barrier, inc=1, device_id=device, device_id_type=MESH)

    here_first = sum(jnp.where(when, 1, 0) for _, when in greeted) + far_greeted

    @pl.when(here_first > 0)
    def _():
        pl.semaphore_wait(barrier, here_first)

    for n, (device, when) in enumerate(greeted):

        @pl.when(when)
        def _():
            pl.semaphore_signal(
                ready_sem.at[mirror[n]], inc=1, device_id=device, device_id_type=MESH
            )

    for device in (at(-9), at(-10)):

        @pl.when(root)
        def _():
            pl.semaphore_signal(ready_sem.at[6], inc=1, device_id=device, device_id_type=MESH)

    @pl.when(end)
    def _():
        pl.semaphore_signal(ready_sem.at[6], inc=1, device_id=at(9), device_id_type=MESH)

    def far_ready():
        @pl.when(jnp.logical_or(far_to_root, jnp.logical_and(z == 4, even)))
        def _():
            pl.semaphore_wait(ready_sem.at[6], 1)

    def ready(n, when):
        @pl.when(jnp.logical_and(greets[n][1], when))
        def _():
            pl.semaphore_wait(ready_sem.at[n], 1)

    sent = []

    def copy_to(src, dst, recv, device, sem):
        return pltpu.make_async_remote_copy(
            src_ref=src,
            dst_ref=dst,
            send_sem=sem,
            recv_sem=recv,
            device_id=device,
            device_id_type=MESH,
        )

    def send(src, dst, recv, device, when):
        copy = copy_to(src, dst, recv, device, send_sem.at[len(sent)])
        sent.append((copy, when))
        pl.when(when)(copy.start)

    def arrived(dst, recv):
        pltpu.make_async_remote_copy(
            src_ref=dst,
            dst_ref=dst,
            send_sem=send_sem.at[0],
            recv_sem=recv,
            device_id=sib,
            device_id_type=MESH,
        ).wait_recv()

    def part(k):
        return pl.ds(pl.multiple_of(k * piece, piece), piece)

    def lane(s, hop, k, core):
        start = pl.multiple_of(core * rows + k * piece, piece)
        return pair.at[s, hop, pl.ds(start, piece), :]

    def send_own(s, when):
        for k in range(CHUNKS):
            send(source[s].at[part(k)], lane(s, 0, k, c), hop_sem.at[s, 0, k], along[s], when)

    def send_cross(s, when):
        ready(4 + s, when)
        send(source[s], cross.at[s], cross_sem.at[s], over[s], when)

    def send_far(width, db, when, block=texts):
        for k in range(CHUNKS):
            dst, recv = width(k)
            send(block.at[part(k)], dst, recv, at(db), when)

    below_root = is_root(along[1])
    late = jnp.logical_or(first, below_root)
    send_far(lambda k: (lane(0, 2, k, c), hop_sem.at[0, 2, k]), 6, jnp.logical_and(z == 5, odd))
    send_far(lambda k: (lane(0, 1, k, c), hop_sem.at[0, 1, k]), 4, z == 6)
    send_own(1, ~late)
    ready(0, g >= 0)
    send_own(0, g >= 0)
    send_far(lambda k: (relay.at[part(k)], relay_sem.at[k]), -4, jnp.logical_and(z == 5, even))
    send_far(lambda k: (relay.at[part(k)], relay_sem.at[k]), -2, jnp.logical_and(z == 4, odd))
    send_far(
        lambda k: (relay.at[part(k)], relay_sem.at[k]), 2, jnp.logical_and(z == 3, even), images
    )
    send(images, ext.at[1], ext_sem.at[1], nextdoor[1], jnp.logical_and(odd, ~first))
    ready(2, even)
    send(texts, ext.at[0], ext_sem.at[0], nextdoor[0], even)
    for s in range(2):
        send_cross(s, jnp.logical_and(inner_up, ~is_root(over[s])))

    def meet(side, block, positive=False, first=False):
        values = block[...]
        dots = lax.dot_general(
            own[side], values, (((1,), (1,)), ((), ())), preferred_element_type=jnp.float32
        )
        score = factor * dots + offset
        if positive:
            diagonal = lax.broadcasted_iota(jnp.int32, score.shape, 0) == lax.broadcasted_iota(
                jnp.int32, score.shape, 1
            )
            score = jnp.where(diagonal, -score, score)
        small = jnp.exp(-jnp.abs(score))
        share = 1.0 / (1.0 + small)
        coef = jnp.where(score >= 0, share, small * share)
        if positive:
            coef = jnp.where(diagonal, -coef, coef)
        term = jnp.maximum(score, 0.0) + jnp.log1p(small)
        if score.shape[1] > rows:
            term = term[:, :rows] + term[:, rows:]
        grad = jnp.dot(coef.astype(jnp.bfloat16), values, preferred_element_type=jnp.float32)
        if first:
            lacc[side] = term
            acc[side] = grad
        else:
            lacc[side] += term
            acc[side] += grad

    for load in loads:
        load.wait()
    factor, offset = scale[0], bias[0]
    for side in range(2):
        meet(side, own.at[1 - side], positive=True, first=True)

    def meet_cross(when):
        @pl.when(when)
        def _():
            for s in range(2):
                arrived(cross.at[s], cross_sem.at[s])

            @pl.loop(0, 2)
            def _(s):
                meet(s, cross.at[s])

    ready(2, odd)
    ready(1, late)
    send_own(1, late)
    ready(3, g >= 0)
    send(images, ext.at[1], ext_sem.at[1], nextdoor[1], jnp.logical_and(odd, first))
    for s in range(2):
        send_cross(s, jnp.logical_and(inner_up, is_root(over[s])))

    by_root = jnp.logical_and(b < 16, g == 0)
    code = jnp.where(jnp.logical_or(first, last), 19, jnp.where(z == 1, 14, jnp.where(z == 2, 26, 42)))
    code = jnp.where(
        jnp.logical_and(by_root, z == 1),
        19,
        jnp.where(jnp.logical_and(by_root, z == 2), 22, jnp.where(jnp.logical_and(by_root, z == 3), 26, code)),
    )

    def stream_hop(i):
        s = lax.rem(code // (1 << i), 2)
        ups = sum(lax.rem(code // (1 << j), 2) for j in range(i)) if i else 0
        return s, jnp.where(s == 1, ups, i - ups)

    steps = [stream_hop(i) for i in range(2 * HOPS)]

    def stays(s):
        return jnp.logical_or(inner_up, s == 1)

    def ends(s):
        return jnp.logical_or(inner_down, s == 0)

    def pass_relay():
        for k in range(CHUNKS):
            here = relay.at[part(k)]
            relays = jnp.logical_or(z == 3, jnp.logical_and(z == 4, even))

            @pl.when(relays)
            def _():
                arrived(here, relay_sem.at[k])

            send(here, lane(0, 2, k, c), hop_sem.at[0, 2, k], at(10), jnp.logical_and(z == 3, even))
            send(here, ext.at[0, part(k)], late_sem(ext_sem, 0, k), at(9), jnp.logical_and(z == 3, odd))
            send(here, ext.at[1, part(k)], late_sem(ext_sem, 1, k), at(-9), jnp.logical_and(z == 4, even))

    def stage(i, k):
        mix = {2: first, 3: first, 4: z == 1, 5: z == 1}.get(i)
        if mix is None:
            return (*steps[i], k)
        base = i - i % 2
        j = (i - base) * CHUNKS + k
        (s0, h0), (s1, h1) = steps[base], steps[base + 1]
        pick = jnp.where(mix, j % 2, i - base)
        return (
            jnp.where(pick == 0, s0, s1),
            jnp.where(pick == 0, h0, h1),
            jnp.where(mix, j // 2, k),
        )

    def forwards(i, k):
        n = i * CHUNKS + k
        s, hop, k = stage(i, k)
        here = lane(s, hop, k, c)
        further = lane(s, lax.rem(hop + 1, HOPS), k, c)
        return (
            (
                copy_to(here, further, hop_sem.at[s, lax.rem(hop + 1, HOPS), k], at(2 - 4 * s), hop_send.at[n, 0]),
                jnp.logical_and(hop + 1 < HOPS, stays(s)),
            ),
            (
                copy_to(here, ext.at[s, part(k)], late_sem(ext_sem, s, k), at(1 - 2 * s), hop_send.at[n, 0]),
                jnp.logical_and(
                    jnp.logical_and(hop + 1 == HOPS, c == 1 - s), jnp.logical_and(stays(s), ends(s))
                ),
            ),
            (copy_to(here, here, sib_sem.at[s, hop, k], sib, hop_send.at[n, 1]), g >= 0),
        )

    for i in range(2 * HOPS + 1):
        if i < 2 * HOPS:
            for k in range(CHUNKS):
                s, hop, p = stage(i, k)
                arrived(lane(s, hop, p, c), hop_sem.at[s, hop, p])
                for copy, when in forwards(i, k):
                    pl.when(when)(copy.start)
        if i == RELAY_AT:
            far_ready()
            pass_relay()
        if i == CROSS_AT:
            for s in range(2):
                send_cross(s, last)
        if i == 1:
            early = 1 - c
            arrived(ext.at[early], ext_sem.at[early])
            meet(early, ext.at[early])
        if i == 3:
            meet_cross(jnp.logical_and(inner_up, inner_down))
        if i >= 1:
            s, hop = steps[i - 1]
            for k in range(CHUNKS):
                arrived(lane(s, hop, k, 1 - c), sib_sem.at[s, hop, k])
            meet(s, pair.at[s, hop])
    meet_cross(jnp.logical_or(first, last))
    for k in range(CHUNKS):
        arrived(ext.at[c, part(k)], late_sem(ext_sem, c, k))
    meet(c, ext.at[c])

    for side in range(2):
        grad_out[side] = factor * acc[side]
    loss_out[...] = jnp.sum(lacc[0].T, axis=0, keepdims=True)
    for copy, when in sent:
        pl.when(when)(copy.wait_send)
    for i in range(2 * HOPS):
        for k in range(CHUNKS):
            for copy, when in forwards(i, k):
                pl.when(when)(copy.wait_send)


def late_sem(ext_sem, s, k):
    return ext_sem.at[2 + 2 * k + s]


def hand_over(loss_in, grad_in, loss_out, gimg_out, gtxt_out, sem):
    half = gimg_out.shape[0] // 2
    copies = [pltpu.make_async_copy(loss_in, loss_out, sem.at[4])]
    for side, out in enumerate((gimg_out, gtxt_out)):
        for k in range(2):
            rows = pl.ds(k * half, half)
            copies.append(
                pltpu.make_async_copy(grad_in.at[side, rows], out.at[rows], sem.at[2 * side + k])
            )
    for copy in copies:
        copy.start()
    for copy in copies:
        copy.wait()


def solution(mesh):
    n_blk, n_grp = mesh.shape["blk"], mesh.shape["grp"]

    def on_device(images, texts, scale, bias):
        rows, width = images.shape
        bf16, f32 = jnp.bfloat16, jnp.float32
        hbm = pl.BlockSpec(memory_space=pltpu.HBM)
        vmem = pl.BlockSpec(memory_space=pltpu.VMEM)
        anywhere = pl.BlockSpec(memory_space=pl.ANY)
        loss, grads = pl.pallas_call(
            functools.partial(kernel, n_blk, n_grp),
            out_shape=(
                jax.ShapeDtypeStruct((1, rows), f32),
                jax.ShapeDtypeStruct((2, rows, width), f32),
            ),
            in_specs=[hbm] * 4,
            out_specs=(vmem, vmem),
            scratch_shapes=[
                pltpu.VMEM((2, rows, width), bf16),
                pltpu.VMEM((2, HOPS, 2 * rows, width), bf16),
                pltpu.VMEM((2, rows, width), bf16),
                pltpu.VMEM((2, rows, width), bf16),
                pltpu.VMEM((2, rows, width), f32),
                pltpu.VMEM((2, rows, rows), f32),
                pltpu.SemaphoreType.DMA((4,)),
                pltpu.VMEM((rows, width), bf16),
                pltpu.SemaphoreType.DMA((CHUNKS,)),
                pltpu.SemaphoreType.DMA((11 * CHUNKS + 9,)),
                pltpu.SemaphoreType.DMA((2 * HOPS * CHUNKS, 2)),
                pltpu.SemaphoreType.DMA((2, HOPS, CHUNKS)),
                pltpu.SemaphoreType.DMA((2, HOPS, CHUNKS)),
                pltpu.SemaphoreType.DMA((2 + 2 * CHUNKS,)),
                pltpu.SemaphoreType.DMA((2,)),
                pltpu.SemaphoreType.REGULAR((7,)),
                pltpu.SMEM((1,), f32),
                pltpu.SMEM((1,), f32),
            ],
            compiler_params=pltpu.CompilerParams(
                collective_id=0, has_side_effects=True, vmem_limit_bytes=VMEM_LIMIT
            ),
        )(images, texts, scale, bias)
        loss, gimg, gtxt = pl.pallas_call(
            hand_over,
            out_shape=(
                jax.ShapeDtypeStruct((1, rows), f32),
                jax.ShapeDtypeStruct((rows, width), f32),
                jax.ShapeDtypeStruct((rows, width), f32),
            ),
            in_specs=[anywhere] * 2,
            out_specs=(anywhere,) * 3,
            scratch_shapes=[pltpu.SemaphoreType.DMA((5,))],
            compiler_params=pltpu.CompilerParams(vmem_limit_bytes=VMEM_LIMIT),
        )(loss, grads)
        return loss.reshape(rows), gimg, gtxt

    block = P(("blk", "grp"), None)
    return jax.shard_map(
        on_device,
        mesh=mesh,
        in_specs=(block, block, P(), P()),
        out_specs=(P(("blk", "grp")), block, block),
        check_vma=False,
    )
```

```python
import functools

import jax
import jax.numpy as jnp
from jax import lax
from jax.experimental import pallas as pl
from jax.experimental.pallas import tpu as pltpu
from jax.sharding import PartitionSpec as P

HOPS = 3
CHUNKS = 2
RELAY_AT = 2
FAR_AT = 0
CROSS_AT = 1
VMEM_LIMIT = 48 * 2**20
MESH = pl.DeviceIdType.MESH


def kernel(
    n_blk,
    n_grp,
    images,
    texts,
    scale_in,
    bias_in,
    loss_out,
    grad_out,
    own,
    pair,
    ext,
    cross,
    acc,
    lacc,
    load_sem,
    relay,
    relay_sem,
    send_sem,
    hop_send,
    hop_sem,
    sib_sem,
    ext_sem,
    cross_sem,
    ready_sem,
    scale,
    bias,
):
    rows = own.shape[1]
    piece = rows // CHUNKS
    b = lax.axis_index("blk")
    g = lax.axis_index("grp")
    c = lax.rem(b, 2)
    z = lax.rem(b // 2, 8)

    def is_root(device):
        return jnp.logical_and(device[0] == 0, device[1] == 0)

    def at(db, dg=0):
        return (lax.rem(b + db + n_blk, n_blk), lax.rem(g + dg + n_grp, n_grp))

    sib = at(1 - 2 * c)
    along = (at(2), at(-2))
    along2 = (at(4), at(-4))
    nextdoor = (at(1), at(-1))
    over = (at(0, 1), at(0, -1))
    source = (texts, images)

    loads = [
        pltpu.make_async_copy(images, own.at[0], load_sem.at[0]),
        pltpu.make_async_copy(texts, own.at[1], load_sem.at[1]),
        pltpu.make_async_copy(scale_in, scale, load_sem.at[2]),
        pltpu.make_async_copy(bias_in, bias, load_sem.at[3]),
    ]
    for load in loads:
        load.start()

    first, last = z == 0, z == 7
    inner_up, inner_down = z != 7, z != 0
    greets = (
        (along[0], inner_up),
        (along[1], first),
        (nextdoor[0], jnp.logical_or(c == 0, inner_up)),
        (nextdoor[1], jnp.logical_and(c == 0, first)),
        (over[0], g < 2),
        (over[1], jnp.logical_or(g == 0, g == 3)),
    )
    greeted = (
        (along[0], last),
        (along[1], inner_down),
        (nextdoor[0], jnp.logical_and(c == 1, last)),
        (nextdoor[1], jnp.logical_or(c == 1, inner_down)),
        (over[0], jnp.logical_or(g == 2, g == 3)),
        (over[1], jnp.logical_or(g == 1, g == 2)),
    )
    mirror = (1, 0, 3, 2, 5, 4)
    root = is_root((b, g))
    def flips(n, to):
        near_root = jnp.logical_and(is_root(to), z != 7)
        return near_root if n in (1, 3) else jnp.logical_or(root, near_root)

    greets = tuple(
        (to, jnp.where(flips(n, to), ~root, when)) for n, (to, when) in enumerate(greets)
    )
    greeted = tuple(
        (to, jnp.where(flips(n, to), root, when)) for n, (to, when) in enumerate(greeted)
    )
    far_to_root = jnp.logical_and(z == 3, jnp.where(c == 0, is_root(at(10)), is_root(at(9))))
    even, odd = c == 0, c == 1
    far_greets = (
        (at(-4), first),
        (at(-6), jnp.logical_and(first, odd)),
        (at(-9), jnp.logical_and(first, jnp.logical_and(even, ~root))),
        (at(-10), jnp.logical_and(first, jnp.logical_and(even, ~root))),
        ((0, 0), far_to_root),
        (at(-9), jnp.logical_and(z == 4, even)),
        (at(4), jnp.logical_and(z == 3, even)),
    )
    end = jnp.logical_and(last, odd)
    far_greeted = jnp.where(
        jnp.logical_or(jnp.logical_or(z == 3, end), jnp.logical_or(z == 5, z == 6)), 1, 0
    )
    far_greeted = jnp.where(far_to_root, 0, jnp.where(root, 2, far_greeted))
    barrier = pltpu.get_barrier_semaphore()
    for device, when in greets + far_greets:

        @pl.when(when)
        def _():
            pl.semaphore_signal(barrier, inc=1, device_id=device, device_id_type=MESH)

    here_first = sum(jnp.where(when, 1, 0) for _, when in greeted) + far_greeted

    @pl.when(here_first > 0)
    def _():
        pl.semaphore_wait(barrier, here_first)

    for n, (device, when) in enumerate(greeted):

        @pl.when(when)
        def _():
            pl.semaphore_signal(
                ready_sem.at[mirror[n]], inc=1, device_id=device, device_id_type=MESH
            )

    for device in (at(-9), at(-10)):

        @pl.when(root)
        def _():
            pl.semaphore_signal(ready_sem.at[6], inc=1, device_id=device, device_id_type=MESH)

    @pl.when(end)
    def _():
        pl.semaphore_signal(ready_sem.at[6], inc=1, device_id=at(9), device_id_type=MESH)

    def far_ready():
        @pl.when(jnp.logical_or(far_to_root, jnp.logical_and(z == 4, even)))
        def _():
            pl.semaphore_wait(ready_sem.at[6], 1)

    def ready(n, when):
        @pl.when(jnp.logical_and(greets[n][1], when))
        def _():
            pl.semaphore_wait(ready_sem.at[n], 1)

    sent = []

    def copy_to(src, dst, recv, device, sem):
        return pltpu.make_async_remote_copy(
            src_ref=src,
            dst_ref=dst,
            send_sem=sem,
            recv_sem=recv,
            device_id=device,
            device_id_type=MESH,
        )

    def send(src, dst, recv, device, when):
        copy = copy_to(src, dst, recv, device, send_sem.at[len(sent)])
        sent.append((copy, when))
        pl.when(when)(copy.start)

    def arrived(dst, recv):
        pltpu.make_async_remote_copy(
            src_ref=dst,
            dst_ref=dst,
            send_sem=send_sem.at[0],
            recv_sem=recv,
            device_id=sib,
            device_id_type=MESH,
        ).wait_recv()

    def part(k):
        return pl.ds(pl.multiple_of(k * piece, piece), piece)

    def lane(s, hop, k, core):
        start = pl.multiple_of(core * rows + k * piece, piece)
        return pair.at[s, hop, pl.ds(start, piece), :]

    def send_own(s, when):
        for k in range(CHUNKS):
            send(source[s].at[part(k)], lane(s, 0, k, c), hop_sem.at[s, 0, k], along[s], when)

    def send_cross(s, when):
        ready(4 + s, when)
        send(source[s], cross.at[s], cross_sem.at[s], over[s], when)

    def send_far(width, db, when, block=texts):
        for k in range(CHUNKS):
            dst, recv = width(k)
            send(block.at[part(k)], dst, recv, at(db), when)

    below_root = is_root(along[1])
    cross_late = z >= 5
    late = jnp.logical_or(first, below_root)
    send_far(lambda k: (lane(0, 2, k, c), hop_sem.at[0, 2, k]), 6, jnp.logical_and(z == 5, odd))
    send_own(1, ~late)
    ready(0, g >= 0)
    send_own(0, g >= 0)
    send_far(lambda k: (relay.at[part(k)], relay_sem.at[k]), -4, jnp.logical_and(z == 5, even))
    send_far(lambda k: (relay.at[part(k)], relay_sem.at[k]), -2, jnp.logical_and(z == 4, odd))
    send(images, ext.at[1], ext_sem.at[1], nextdoor[1], jnp.logical_and(odd, ~first))
    ready(2, even)
    send(texts, ext.at[0], ext_sem.at[0], nextdoor[0], even)
    for s in range(2):
        send_cross(s, jnp.logical_and(~cross_late, ~is_root(over[s])))

    def meet(pairs, positive=False):
        values = [block[...] for _, block in pairs]
        scores = [
            factor
            * lax.dot_general(
                own[side], value, (((1,), (1,)), ((), ())), preferred_element_type=jnp.float32
            )
            + offset
            for (side, _), value in zip(pairs, values)
        ]
        coefs, terms = [], []
        for score in scores:
            if positive:
                diagonal = lax.broadcasted_iota(jnp.int32, score.shape, 0) == lax.broadcasted_iota(
                    jnp.int32, score.shape, 1
                )
                score = jnp.where(diagonal, -score, score)
            small = jnp.exp(-jnp.abs(score))
            share = 1.0 / (1.0 + small)
            coef = jnp.where(score >= 0, share, small * share)
            if positive:
                coef = jnp.where(diagonal, -coef, coef)
            term = jnp.maximum(score, 0.0) + jnp.log1p(small)
            if score.shape[1] > rows:
                term = term[:, :rows] + term[:, rows:]
            coefs.append(coef.astype(jnp.bfloat16))
            terms.append(term)
        grads = [
            jnp.dot(coef, value, preferred_element_type=jnp.float32)
            for coef, value in zip(coefs, values)
        ]
        for (side, _), term, grad in zip(pairs, terms, grads):
            if positive:
                lacc[side] = term
                acc[side] = grad
            else:
                lacc[side] += term
                acc[side] += grad

    for load in loads:
        load.wait()
    factor, offset = scale[0], bias[0]
    meet([(side, own.at[1 - side]) for side in range(2)], positive=True)

    def meet_cross(when):
        @pl.when(when)
        def _():
            for s in range(2):
                arrived(cross.at[s], cross_sem.at[s])
            early = 1 - c
            arrived(ext.at[early], ext_sem.at[early])
            meet([(0, cross.at[0]), (1, cross.at[1]), (early, ext.at[early])])

    ready(2, odd)
    ready(1, late)
    send_own(1, late)
    ready(3, g >= 0)
    send(images, ext.at[1], ext_sem.at[1], nextdoor[1], jnp.logical_and(odd, first))
    for s in range(2):
        send_cross(s, jnp.logical_and(~cross_late, is_root(over[s])))

    by_root = jnp.logical_and(b < 16, g == 0)
    code = jnp.where(
        first,
        jnp.where(even, 19, 35),
        jnp.where(last, 19, jnp.where(z == 1, jnp.where(even, 14, 38), jnp.where(even, 26, 42))),
    )
    code = jnp.where(
        jnp.logical_and(by_root, z == 1),
        19,
        jnp.where(jnp.logical_and(by_root, z == 2), 22, jnp.where(jnp.logical_and(by_root, z == 3), 26, code)),
    )

    def stream_hop(i):
        s = lax.rem(code // (1 << i), 2)
        ups = sum(lax.rem(code // (1 << j), 2) for j in range(i)) if i else 0
        return s, jnp.where(s == 1, ups, i - ups)

    steps = [stream_hop(i) for i in range(2 * HOPS)]

    def stays(s):
        return jnp.logical_or(inner_up, s == 1)

    def ends(s):
        return jnp.logical_or(inner_down, s == 0)

    def pass_relay(when):
        for k in range(CHUNKS):
            here = relay.at[part(k)]
            relays = jnp.logical_and(when, jnp.logical_or(z == 3, even))

            @pl.when(relays)
            def _():
                arrived(here, relay_sem.at[k])

            send(here, lane(0, 2, k, c), hop_sem.at[0, 2, k], at(10), jnp.logical_and(jnp.logical_and(when, z == 3), even))
            send(here, ext.at[0, part(k)], late_sem(ext_sem, 0, k), at(9), jnp.logical_and(jnp.logical_and(when, z == 3), odd))
            send(here, ext.at[1, part(k)], late_sem(ext_sem, 1, k), at(-9), jnp.logical_and(jnp.logical_and(when, z == 4), even))

    def stage(i, k):
        mix = None
        if mix is None:
            return (*steps[i], k)
        base = i - i % 2
        j = (i - base) * CHUNKS + k
        (s0, h0), (s1, h1) = steps[base], steps[base + 1]
        pick = jnp.where(mix, j % 2, i - base)
        return (
            jnp.where(pick == 0, s0, s1),
            jnp.where(pick == 0, h0, h1),
            jnp.where(mix, j // 2, k),
        )

    def forwards(i, k):
        n = i * CHUNKS + k
        s, hop, k = stage(i, k)
        here = lane(s, hop, k, c)
        further = lane(s, lax.rem(hop + 1, HOPS), k, c)
        return (
            (
                copy_to(here, further, hop_sem.at[s, lax.rem(hop + 1, HOPS), k], at(2 - 4 * s), hop_send.at[n, 0]),
                jnp.logical_and(hop + 1 < HOPS, stays(s)),
            ),
            (
                copy_to(here, ext.at[s, part(k)], late_sem(ext_sem, s, k), at(1 - 2 * s), hop_send.at[n, 0]),
                jnp.logical_and(
                    jnp.logical_and(hop + 1 == HOPS, c == 1 - s), jnp.logical_and(stays(s), ends(s))
                ),
            ),
            (copy_to(here, here, sib_sem.at[s, hop, k], sib, hop_send.at[n, 1]), g >= 0),
        )

    for i in range(2 * HOPS + 1):
        if i < 2 * HOPS:
            for k in range(CHUNKS):
                s, hop, p = stage(i, k)
                arrived(lane(s, hop, p, c), hop_sem.at[s, hop, p])
                if i == 0 and k == 0:
                    send_far(lambda k: (lane(0, 1, k, c), hop_sem.at[0, 1, k]), 4, z == 6)
                for copy, when in forwards(i, k):
                    pl.when(when)(copy.start)
        if i == RELAY_AT:
            send_far(
                lambda k: (relay.at[part(k)], relay_sem.at[k]), 2, jnp.logical_and(z == 3, even), images
            )
            far_ready()
            pass_relay(z == 3)
        if i == RELAY_AT + 2:
            pass_relay(z == 4)
        if i == CROSS_AT:
            for s in range(2):
                send_cross(s, cross_late)
        if i == 3:
            meet_cross(jnp.logical_and(~cross_late, inner_down))
        if i in (2, 4, 6):
            for s, hop in steps[i - 2 : i]:
                for k in range(CHUNKS):
                    arrived(lane(s, hop, k, 1 - c), sib_sem.at[s, hop, k])
            meet([(s, pair.at[s, hop]) for s, hop in steps[i - 2 : i]])
    meet_cross(jnp.logical_or(first, cross_late))
    for k in range(CHUNKS):
        arrived(ext.at[c, part(k)], late_sem(ext_sem, c, k))
    meet([(c, ext.at[c])])

    for side in range(2):
        grad_out[side] = factor * acc[side]
    loss_out[...] = jnp.sum(lacc[0].T, axis=0, keepdims=True)
    for copy, when in sent:
        pl.when(when)(copy.wait_send)
    for i in range(2 * HOPS):
        for k in range(CHUNKS):
            for copy, when in forwards(i, k):
                pl.when(when)(copy.wait_send)


def late_sem(ext_sem, s, k):
    return ext_sem.at[2 + 2 * k + s]


def hand_over(loss_in, grad_in, loss_out, gimg_out, gtxt_out, sem):
    half = gimg_out.shape[0] // 2
    copies = [pltpu.make_async_copy(loss_in, loss_out, sem.at[4])]
    for side, out in enumerate((gimg_out, gtxt_out)):
        for k in range(2):
            rows = pl.ds(k * half, half)
            copies.append(
                pltpu.make_async_copy(grad_in.at[side, rows], out.at[rows], sem.at[2 * side + k])
            )
    for copy in copies:
        copy.start()
    for copy in copies:
        copy.wait()


def solution(mesh):
    n_blk, n_grp = mesh.shape["blk"], mesh.shape["grp"]

    def on_device(images, texts, scale, bias):
        rows, width = images.shape
        bf16, f32 = jnp.bfloat16, jnp.float32
        hbm = pl.BlockSpec(memory_space=pltpu.HBM)
        vmem = pl.BlockSpec(memory_space=pltpu.VMEM)
        anywhere = pl.BlockSpec(memory_space=pl.ANY)
        loss, grads = pl.pallas_call(
            functools.partial(kernel, n_blk, n_grp),
            out_shape=(
                jax.ShapeDtypeStruct((1, rows), f32),
                jax.ShapeDtypeStruct((2, rows, width), f32),
            ),
            in_specs=[vmem, vmem, hbm, hbm],
            out_specs=(vmem, vmem),
            scratch_shapes=[
                pltpu.VMEM((2, rows, width), bf16),
                pltpu.VMEM((2, HOPS, 2 * rows, width), bf16),
                pltpu.VMEM((2, rows, width), bf16),
                pltpu.VMEM((2, rows, width), bf16),
                pltpu.VMEM((2, rows, width), f32),
                pltpu.VMEM((2, rows, rows), f32),
                pltpu.SemaphoreType.DMA((4,)),
                pltpu.VMEM((rows, width), bf16),
                pltpu.SemaphoreType.DMA((CHUNKS,)),
                pltpu.SemaphoreType.DMA((14 * CHUNKS + 9,)),
                pltpu.SemaphoreType.DMA((2 * HOPS * CHUNKS, 2)),
                pltpu.SemaphoreType.DMA((2, HOPS, CHUNKS)),
                pltpu.SemaphoreType.DMA((2, HOPS, CHUNKS)),
                pltpu.SemaphoreType.DMA((2 + 2 * CHUNKS,)),
                pltpu.SemaphoreType.DMA((2,)),
                pltpu.SemaphoreType.REGULAR((7,)),
                pltpu.SMEM((1,), f32),
                pltpu.SMEM((1,), f32),
            ],
            compiler_params=pltpu.CompilerParams(
                collective_id=0, has_side_effects=True, vmem_limit_bytes=VMEM_LIMIT
            ),
        )(images, texts, scale, bias)
        loss, gimg, gtxt = pl.pallas_call(
            hand_over,
            out_shape=(
                jax.ShapeDtypeStruct((1, rows), f32),
                jax.ShapeDtypeStruct((rows, width), f32),
                jax.ShapeDtypeStruct((rows, width), f32),
            ),
            in_specs=[anywhere] * 2,
            out_specs=(anywhere,) * 3,
            scratch_shapes=[pltpu.SemaphoreType.DMA((5,))],
            compiler_params=pltpu.CompilerParams(vmem_limit_bytes=VMEM_LIMIT),
        )(loss, grads)
        return loss.reshape(rows), gimg, gtxt

    block = P(("blk", "grp"), None)
    return jax.shard_map(
        on_device,
        mesh=mesh,
        in_specs=(block, block, P(), P()),
        out_specs=(P(("blk", "grp")), block, block),
        check_vma=False,
    )
```

```python
import functools

import jax
import jax.numpy as jnp
from jax import lax
from jax.experimental import pallas as pl
from jax.experimental.pallas import tpu as pltpu
from jax.sharding import PartitionSpec as P

HOPS = 3
CHUNKS = 2
RELAY_AT = 2
FAR_AT = 0
CROSS_AT = 2
VMEM_LIMIT = 48 * 2**20
MESH = pl.DeviceIdType.MESH


def kernel(
    n_blk,
    n_grp,
    own,
    scale_in,
    bias_in,
    loss_out,
    grad_out,
    pair,
    ext,
    cross,
    acc,
    lacc,
    load_sem,
    relay,
    relay_sem,
    send_sem,
    hop_send,
    hop_sem,
    sib_sem,
    ext_sem,
    cross_sem,
    ready_sem,
    scale,
    bias,
):
    rows = own.shape[1]
    piece = rows // CHUNKS
    b = lax.axis_index("blk")
    g = lax.axis_index("grp")
    c = lax.rem(b, 2)
    z = lax.rem(b // 2, 8)

    def is_root(device):
        return jnp.logical_and(device[0] == 0, device[1] == 0)

    def at(db, dg=0):
        return (lax.rem(b + db + n_blk, n_blk), lax.rem(g + dg + n_grp, n_grp))

    sib = at(1 - 2 * c)
    along = (at(2), at(-2))
    along2 = (at(4), at(-4))
    nextdoor = (at(1), at(-1))
    over = (at(0, 1), at(0, -1))
    images, texts = own.at[0], own.at[1]
    source = (texts, images)

    loads = [
        pltpu.make_async_copy(scale_in, scale, load_sem.at[0]),
        pltpu.make_async_copy(bias_in, bias, load_sem.at[1]),
    ]
    for load in loads:
        load.start()

    first, last = z == 0, z == 7
    inner_up, inner_down = z != 7, z != 0
    greets = (
        (along[0], inner_up),
        (along[1], first),
        (nextdoor[0], jnp.logical_or(c == 0, inner_up)),
        (nextdoor[1], jnp.logical_and(c == 0, first)),
        (over[0], g < 2),
        (over[1], jnp.logical_or(g == 0, g == 3)),
    )
    greeted = (
        (along[0], last),
        (along[1], inner_down),
        (nextdoor[0], jnp.logical_and(c == 1, last)),
        (nextdoor[1], jnp.logical_or(c == 1, inner_down)),
        (over[0], jnp.logical_or(g == 2, g == 3)),
        (over[1], jnp.logical_or(g == 1, g == 2)),
    )
    mirror = (1, 0, 3, 2, 5, 4)
    root = is_root((b, g))
    def flips(n, to):
        near_root = jnp.logical_and(is_root(to), z != 7)
        return near_root if n in (1, 3) else jnp.logical_or(root, near_root)

    greets = tuple(
        (to, jnp.where(flips(n, to), ~root, when)) for n, (to, when) in enumerate(greets)
    )
    greeted = tuple(
        (to, jnp.where(flips(n, to), root, when)) for n, (to, when) in enumerate(greeted)
    )
    far_to_root = jnp.logical_and(z == 3, jnp.where(c == 0, is_root(at(10)), is_root(at(9))))
    even, odd = c == 0, c == 1
    far_greets = (
        (at(-4), first),
        (at(-6), jnp.logical_and(first, odd)),
        (at(-9), jnp.logical_and(first, jnp.logical_and(even, ~root))),
        (at(-10), jnp.logical_and(first, jnp.logical_and(even, ~root))),
        ((0, 0), far_to_root),
        (at(-9), jnp.logical_and(z == 4, even)),
        (at(4), jnp.logical_and(z == 3, even)),
    )
    end = jnp.logical_and(last, odd)
    far_greeted = jnp.where(
        jnp.logical_or(jnp.logical_or(z == 3, end), jnp.logical_or(z == 5, z == 6)), 1, 0
    )
    far_greeted = jnp.where(far_to_root, 0, jnp.where(root, 2, far_greeted))
    barrier = pltpu.get_barrier_semaphore()
    for device, when in greets + far_greets:

        @pl.when(when)
        def _():
            pl.semaphore_signal(barrier, inc=1, device_id=device, device_id_type=MESH)

    here_first = sum(jnp.where(when, 1, 0) for _, when in greeted) + far_greeted

    @pl.when(here_first > 0)
    def _():
        pl.semaphore_wait(barrier, here_first)

    for n, (device, when) in enumerate(greeted):

        @pl.when(when)
        def _():
            pl.semaphore_signal(
                ready_sem.at[mirror[n]], inc=1, device_id=device, device_id_type=MESH
            )

    for device in (at(-9), at(-10)):

        @pl.when(root)
        def _():
            pl.semaphore_signal(ready_sem.at[6], inc=1, device_id=device, device_id_type=MESH)

    @pl.when(end)
    def _():
        pl.semaphore_signal(ready_sem.at[6], inc=1, device_id=at(9), device_id_type=MESH)

    def far_ready():
        @pl.when(jnp.logical_or(far_to_root, jnp.logical_and(z == 4, even)))
        def _():
            pl.semaphore_wait(ready_sem.at[6], 1)

    def ready(n, when):
        @pl.when(jnp.logical_and(greets[n][1], when))
        def _():
            pl.semaphore_wait(ready_sem.at[n], 1)

    sent = []

    def copy_to(src, dst, recv, device, sem):
        return pltpu.make_async_remote_copy(
            src_ref=src,
            dst_ref=dst,
            send_sem=sem,
            recv_sem=recv,
            device_id=device,
            device_id_type=MESH,
        )

    def send(src, dst, recv, device, when):
        copy = copy_to(src, dst, recv, device, send_sem.at[len(sent)])
        sent.append((copy, when))
        pl.when(when)(copy.start)

    def arrived(dst, recv):
        pltpu.make_async_remote_copy(
            src_ref=dst,
            dst_ref=dst,
            send_sem=send_sem.at[0],
            recv_sem=recv,
            device_id=sib,
            device_id_type=MESH,
        ).wait_recv()

    def part(k):
        return pl.ds(pl.multiple_of(k * piece, piece), piece)

    def lane(s, hop, k, core):
        start = pl.multiple_of(core * rows + k * piece, piece)
        return pair.at[s, hop, pl.ds(start, piece), :]

    def send_own(s, when):
        for k in range(CHUNKS):
            send(source[s].at[part(k)], lane(s, 0, k, c), hop_sem.at[s, 0, k], along[s], when)

    def send_cross(s, when):
        ready(4 + s, when)
        send(source[s], cross.at[s], cross_sem.at[s], over[s], when)

    def send_far(width, db, when, block=texts):
        for k in range(CHUNKS):
            dst, recv = width(k)
            send(block.at[part(k)], dst, recv, at(db), when)

    below_root = is_root(along[1])
    cross_late = z >= 5
    late = jnp.logical_or(first, below_root)
    send_far(lambda k: (lane(0, 2, k, c), hop_sem.at[0, 2, k]), 6, jnp.logical_and(z == 5, odd))
    send_own(1, ~late)
    ready(0, g >= 0)
    send_own(0, g >= 0)
    send_far(lambda k: (relay.at[part(k)], relay_sem.at[k]), -4, jnp.logical_and(z == 5, even))
    send_far(lambda k: (relay.at[part(k)], relay_sem.at[k]), -2, jnp.logical_and(z == 4, odd))
    send(images, ext.at[1], ext_sem.at[1], nextdoor[1], jnp.logical_and(odd, ~first))
    ready(2, even)
    send(texts, ext.at[0], ext_sem.at[0], nextdoor[0], even)
    for s in range(2):
        send_cross(s, jnp.logical_and(~cross_late, ~is_root(over[s])))

    def meet(pairs, positive=False):
        values = [block[...] for _, block in pairs]
        scores = [
            factor
            * lax.dot_general(
                own[side], value, (((1,), (1,)), ((), ())), preferred_element_type=jnp.float32
            )
            + offset
            for (side, _), value in zip(pairs, values)
        ]
        coefs, terms = [], []
        for score in scores:
            if positive:
                diagonal = lax.broadcasted_iota(jnp.int32, score.shape, 0) == lax.broadcasted_iota(
                    jnp.int32, score.shape, 1
                )
                score = jnp.where(diagonal, -score, score)
            small = jnp.exp(-jnp.abs(score))
            share = 1.0 / (1.0 + small)
            coef = jnp.where(score >= 0, share, small * share)
            if positive:
                coef = jnp.where(diagonal, -coef, coef)
            term = jnp.maximum(score, 0.0) + jnp.log1p(small)
            if score.shape[1] > rows:
                term = term[:, :rows] + term[:, rows:]
            coefs.append(coef.astype(jnp.bfloat16))
            terms.append(term)
        grads = [
            jnp.dot(coef, value, preferred_element_type=jnp.float32)
            for coef, value in zip(coefs, values)
        ]
        for (side, _), term, grad in zip(pairs, terms, grads):
            if positive:
                lacc[side] = term
                acc[side] = grad
            else:
                lacc[side] += term
                acc[side] += grad

    for load in loads:
        load.wait()
    factor, offset = scale[0], bias[0]
    meet([(side, own.at[1 - side]) for side in range(2)], positive=True)

    def meet_cross(when):
        @pl.when(when)
        def _():
            for s in range(2):
                arrived(cross.at[s], cross_sem.at[s])
            early = 1 - c
            arrived(ext.at[early], ext_sem.at[early])
            meet([(0, cross.at[0]), (1, cross.at[1]), (early, ext.at[early])])

    ready(2, odd)
    ready(1, late)
    send_own(1, late)
    ready(3, g >= 0)
    send(images, ext.at[1], ext_sem.at[1], nextdoor[1], jnp.logical_and(odd, first))
    for s in range(2):
        send_cross(s, jnp.logical_and(~cross_late, is_root(over[s])))

    by_root = jnp.logical_and(b < 16, g == 0)
    code = jnp.where(
        first,
        jnp.where(even, 19, 35),
        jnp.where(last, 19, jnp.where(z == 1, jnp.where(even, 14, 38), jnp.where(even, 26, 42))),
    )
    code = jnp.where(
        jnp.logical_and(by_root, z == 1),
        19,
        jnp.where(jnp.logical_and(by_root, z == 2), 22, jnp.where(jnp.logical_and(by_root, z == 3), 26, code)),
    )

    def stream_hop(i):
        s = lax.rem(code // (1 << i), 2)
        ups = sum(lax.rem(code // (1 << j), 2) for j in range(i)) if i else 0
        return s, jnp.where(s == 1, ups, i - ups)

    steps = [stream_hop(i) for i in range(2 * HOPS)]

    def stays(s):
        return jnp.logical_or(inner_up, s == 1)

    def ends(s):
        return jnp.logical_or(inner_down, s == 0)

    def pass_relay(when):
        for k in range(CHUNKS):
            here = relay.at[part(k)]
            relays = jnp.logical_and(when, jnp.logical_or(z == 3, even))

            @pl.when(relays)
            def _():
                arrived(here, relay_sem.at[k])

            send(here, lane(0, 2, k, c), hop_sem.at[0, 2, k], at(10), jnp.logical_and(jnp.logical_and(when, z == 3), even))
            send(here, ext.at[0, part(k)], late_sem(ext_sem, 0, k), at(9), jnp.logical_and(jnp.logical_and(when, z == 3), odd))
            send(here, ext.at[1, part(k)], late_sem(ext_sem, 1, k), at(-9), jnp.logical_and(jnp.logical_and(when, z == 4), even))

    def stage(i, k):
        mix = None
        if mix is None:
            return (*steps[i], k)
        base = i - i % 2
        j = (i - base) * CHUNKS + k
        (s0, h0), (s1, h1) = steps[base], steps[base + 1]
        pick = jnp.where(mix, j % 2, i - base)
        return (
            jnp.where(pick == 0, s0, s1),
            jnp.where(pick == 0, h0, h1),
            jnp.where(mix, j // 2, k),
        )

    def forwards(i, k):
        n = i * CHUNKS + k
        s, hop, k = stage(i, k)
        here = lane(s, hop, k, c)
        further = lane(s, lax.rem(hop + 1, HOPS), k, c)
        return (
            (
                copy_to(here, further, hop_sem.at[s, lax.rem(hop + 1, HOPS), k], at(2 - 4 * s), hop_send.at[n, 0]),
                jnp.logical_and(hop + 1 < HOPS, stays(s)),
            ),
            (
                copy_to(here, ext.at[s, part(k)], late_sem(ext_sem, s, k), at(1 - 2 * s), hop_send.at[n, 0]),
                jnp.logical_and(
                    jnp.logical_and(hop + 1 == HOPS, c == 1 - s), jnp.logical_and(stays(s), ends(s))
                ),
            ),
            (copy_to(here, here, sib_sem.at[s, hop, k], sib, hop_send.at[n, 1]), g >= 0),
        )

    for i in range(2 * HOPS + 1):
        if i < 2 * HOPS:
            for k in range(CHUNKS):
                s, hop, p = stage(i, k)
                arrived(lane(s, hop, p, c), hop_sem.at[s, hop, p])
                if i == 0 and k == 0:
                    send_far(lambda k: (lane(0, 1, k, c), hop_sem.at[0, 1, k]), 4, z == 6)
                for copy, when in forwards(i, k):
                    pl.when(when)(copy.start)
        if i == RELAY_AT:
            send_far(
                lambda k: (relay.at[part(k)], relay_sem.at[k]), 2, jnp.logical_and(z == 3, even), images
            )
            far_ready()
            pass_relay(z == 3)
        if i == RELAY_AT + 2:
            pass_relay(z == 4)
        if i == CROSS_AT:
            for s in range(2):
                send_cross(s, cross_late)
        if i == 3:
            meet_cross(jnp.logical_and(~cross_late, inner_down))
        if i in (2, 4, 6):
            for s, hop in steps[i - 2 : i]:
                for k in range(CHUNKS):
                    arrived(lane(s, hop, k, 1 - c), sib_sem.at[s, hop, k])
            meet([(s, pair.at[s, hop]) for s, hop in steps[i - 2 : i]])
    meet_cross(jnp.logical_or(first, cross_late))
    for k in range(CHUNKS):
        arrived(ext.at[c, part(k)], late_sem(ext_sem, c, k))
    meet([(c, ext.at[c])])

    for side in range(2):
        grad_out[side] = factor * acc[side]
    loss_out[...] = jnp.sum(lacc[0].T, axis=0, keepdims=True)
    for copy, when in sent:
        pl.when(when)(copy.wait_send)
    for i in range(2 * HOPS):
        for k in range(CHUNKS):
            for copy, when in forwards(i, k):
                pl.when(when)(copy.wait_send)


def late_sem(ext_sem, s, k):
    return ext_sem.at[2 + 2 * k + s]


def hand_over(loss_in, grad_in, loss_out, gimg_out, gtxt_out, sem):
    half = gimg_out.shape[0] // 2
    copies = [pltpu.make_async_copy(loss_in, loss_out, sem.at[4])]
    for side, out in enumerate((gimg_out, gtxt_out)):
        for k in range(2):
            rows = pl.ds(k * half, half)
            copies.append(
                pltpu.make_async_copy(grad_in.at[side, rows], out.at[rows], sem.at[2 * side + k])
            )
    for copy in copies:
        copy.start()
    for copy in copies:
        copy.wait()


def solution(mesh):
    n_blk, n_grp = mesh.shape["blk"], mesh.shape["grp"]

    def on_device(images, texts, scale, bias):
        rows, width = images.shape
        bf16, f32 = jnp.bfloat16, jnp.float32
        hbm = pl.BlockSpec(memory_space=pltpu.HBM)
        vmem = pl.BlockSpec(memory_space=pltpu.VMEM)
        anywhere = pl.BlockSpec(memory_space=pl.ANY)
        loss, grads = pl.pallas_call(
            functools.partial(kernel, n_blk, n_grp),
            out_shape=(
                jax.ShapeDtypeStruct((1, rows), f32),
                jax.ShapeDtypeStruct((2, rows, width), f32),
            ),
            in_specs=[vmem, hbm, hbm],
            out_specs=(vmem, vmem),
            scratch_shapes=[
                pltpu.VMEM((2, HOPS, 2 * rows, width), bf16),
                pltpu.VMEM((2, rows, width), bf16),
                pltpu.VMEM((2, rows, width), bf16),
                pltpu.VMEM((2, rows, width), f32),
                pltpu.VMEM((2, rows, rows), f32),
                pltpu.SemaphoreType.DMA((2,)),
                pltpu.VMEM((rows, width), bf16),
                pltpu.SemaphoreType.DMA((CHUNKS,)),
                pltpu.SemaphoreType.DMA((14 * CHUNKS + 9,)),
                pltpu.SemaphoreType.DMA((2 * HOPS * CHUNKS, 2)),
                pltpu.SemaphoreType.DMA((2, HOPS, CHUNKS)),
                pltpu.SemaphoreType.DMA((2, HOPS, CHUNKS)),
                pltpu.SemaphoreType.DMA((2 + 2 * CHUNKS,)),
                pltpu.SemaphoreType.DMA((2,)),
                pltpu.SemaphoreType.REGULAR((7,)),
                pltpu.SMEM((1,), f32),
                pltpu.SMEM((1,), f32),
            ],
            compiler_params=pltpu.CompilerParams(
                collective_id=0, has_side_effects=True, vmem_limit_bytes=VMEM_LIMIT
            ),
        )(jnp.stack((images, texts)), scale, bias)
        loss, gimg, gtxt = pl.pallas_call(
            hand_over,
            out_shape=(
                jax.ShapeDtypeStruct((1, rows), f32),
                jax.ShapeDtypeStruct((rows, width), f32),
                jax.ShapeDtypeStruct((rows, width), f32),
            ),
            in_specs=[anywhere] * 2,
            out_specs=(anywhere,) * 3,
            scratch_shapes=[pltpu.SemaphoreType.DMA((5,))],
            compiler_params=pltpu.CompilerParams(vmem_limit_bytes=VMEM_LIMIT),
        )(loss, grads)
        return loss.reshape(rows), gimg, gtxt

    block = P(("blk", "grp"), None)
    return jax.shard_map(
        on_device,
        mesh=mesh,
        in_specs=(block, block, P(), P()),
        out_specs=(P(("blk", "grp")), block, block),
        check_vma=False,
    )
```

```python
import functools

import jax
import jax.numpy as jnp
from jax import lax
from jax.experimental import pallas as pl
from jax.experimental.pallas import tpu as pltpu
from jax.sharding import PartitionSpec as P

HOPS = 3
CHUNKS = 4
RELAY_AT = 2
FAR_AT = 0
CROSS_AT = 2
VMEM_LIMIT = 48 * 2**20
MESH = pl.DeviceIdType.MESH


def kernel(
    n_blk,
    n_grp,
    own,
    scale_in,
    bias_in,
    loss_out,
    grad_out,
    pair,
    ext,
    cross,
    acc,
    lacc,
    load_sem,
    relay,
    relay_sem,
    send_sem,
    hop_send,
    hop_sem,
    sib_sem,
    ext_sem,
    cross_sem,
    ready_sem,
    scale,
    bias,
):
    rows = own.shape[1]
    piece = rows // CHUNKS
    b = lax.axis_index("blk")
    g = lax.axis_index("grp")
    c = lax.rem(b, 2)
    z = lax.rem(b // 2, 8)

    def is_root(device):
        return jnp.logical_and(device[0] == 0, device[1] == 0)

    def at(db, dg=0):
        return (lax.rem(b + db + n_blk, n_blk), lax.rem(g + dg + n_grp, n_grp))

    sib = at(1 - 2 * c)
    along = (at(2), at(-2))
    along2 = (at(4), at(-4))
    nextdoor = (at(1), at(-1))
    over = (at(0, 1), at(0, -1))
    images, texts = own.at[0], own.at[1]
    source = (texts, images)

    loads = [
        pltpu.make_async_copy(scale_in, scale, load_sem.at[0]),
        pltpu.make_async_copy(bias_in, bias, load_sem.at[1]),
    ]
    for load in loads:
        load.start()

    first, last = z == 0, z == 7
    inner_up, inner_down = z != 7, z != 0
    greets = (
        (along[0], inner_up),
        (along[1], first),
        (nextdoor[0], jnp.logical_or(c == 0, inner_up)),
        (nextdoor[1], jnp.logical_and(c == 0, first)),
        (over[0], g < 2),
        (over[1], jnp.logical_or(g == 0, g == 3)),
    )
    greeted = (
        (along[0], last),
        (along[1], inner_down),
        (nextdoor[0], jnp.logical_and(c == 1, last)),
        (nextdoor[1], jnp.logical_or(c == 1, inner_down)),
        (over[0], jnp.logical_or(g == 2, g == 3)),
        (over[1], jnp.logical_or(g == 1, g == 2)),
    )
    mirror = (1, 0, 3, 2, 5, 4)
    root = is_root((b, g))
    def flips(n, to):
        near_root = jnp.logical_and(is_root(to), z != 7)
        return near_root if n in (1, 3) else jnp.logical_or(root, near_root)

    greets = tuple(
        (to, jnp.where(flips(n, to), ~root, when)) for n, (to, when) in enumerate(greets)
    )
    greeted = tuple(
        (to, jnp.where(flips(n, to), root, when)) for n, (to, when) in enumerate(greeted)
    )
    far_to_root = jnp.logical_and(z == 3, jnp.where(c == 0, is_root(at(10)), is_root(at(9))))
    even, odd = c == 0, c == 1
    far_greets = (
        (at(-4), first),
        (at(-6), jnp.logical_and(first, odd)),
        (at(-9), jnp.logical_and(first, jnp.logical_and(even, ~root))),
        (at(-10), jnp.logical_and(first, jnp.logical_and(even, ~root))),
        ((0, 0), far_to_root),
        (at(-9), jnp.logical_and(z == 4, even)),
        (at(4), jnp.logical_and(z == 3, even)),
    )
    end = jnp.logical_and(last, odd)
    far_greeted = jnp.where(
        jnp.logical_or(jnp.logical_or(z == 3, end), jnp.logical_or(z == 5, z == 6)), 1, 0
    )
    far_greeted = jnp.where(far_to_root, 0, jnp.where(root, 2, far_greeted))
    barrier = pltpu.get_barrier_semaphore()
    for device, when in greets + far_greets:

        @pl.when(when)
        def _():
            pl.semaphore_signal(barrier, inc=1, device_id=device, device_id_type=MESH)

    here_first = sum(jnp.where(when, 1, 0) for _, when in greeted) + far_greeted

    @pl.when(here_first > 0)
    def _():
        pl.semaphore_wait(barrier, here_first)

    for n, (device, when) in enumerate(greeted):

        @pl.when(when)
        def _():
            pl.semaphore_signal(
                ready_sem.at[mirror[n]], inc=1, device_id=device, device_id_type=MESH
            )

    for device in (at(-9), at(-10)):

        @pl.when(root)
        def _():
            pl.semaphore_signal(ready_sem.at[6], inc=1, device_id=device, device_id_type=MESH)

    @pl.when(end)
    def _():
        pl.semaphore_signal(ready_sem.at[6], inc=1, device_id=at(9), device_id_type=MESH)

    def far_ready():
        @pl.when(jnp.logical_or(far_to_root, jnp.logical_and(z == 4, even)))
        def _():
            pl.semaphore_wait(ready_sem.at[6], 1)

    def ready(n, when):
        @pl.when(jnp.logical_and(greets[n][1], when))
        def _():
            pl.semaphore_wait(ready_sem.at[n], 1)

    sent = []

    def copy_to(src, dst, recv, device, sem):
        return pltpu.make_async_remote_copy(
            src_ref=src,
            dst_ref=dst,
            send_sem=sem,
            recv_sem=recv,
            device_id=device,
            device_id_type=MESH,
        )

    def send(src, dst, recv, device, when):
        copy = copy_to(src, dst, recv, device, send_sem.at[len(sent)])
        sent.append((copy, when))
        pl.when(when)(copy.start)

    def arrived(dst, recv):
        pltpu.make_async_remote_copy(
            src_ref=dst,
            dst_ref=dst,
            send_sem=send_sem.at[0],
            recv_sem=recv,
            device_id=sib,
            device_id_type=MESH,
        ).wait_recv()

    def part(k):
        return pl.ds(pl.multiple_of(k * piece, piece), piece)

    def lane(s, hop, k, core):
        start = pl.multiple_of(core * rows + k * piece, piece)
        return pair.at[s, hop, pl.ds(start, piece), :]

    def send_own(s, when):
        for k in range(CHUNKS):
            send(source[s].at[part(k)], lane(s, 0, k, c), hop_sem.at[s, 0, k], along[s], when)

    def send_cross(s, when):
        ready(4 + s, when)
        send(source[s], cross.at[s], cross_sem.at[s], over[s], when)

    def send_far(width, db, when, block=texts):
        for k in range(CHUNKS):
            dst, recv = width(k)
            send(block.at[part(k)], dst, recv, at(db), when)

    below_root = is_root(along[1])
    cross_late = z >= 5
    late = jnp.logical_or(first, below_root)
    send_far(lambda k: (lane(0, 2, k, c), hop_sem.at[0, 2, k]), 6, jnp.logical_and(z == 5, odd))
    send_own(1, ~late)
    ready(0, g >= 0)
    send_own(0, g >= 0)
    send_far(lambda k: (relay.at[part(k)], relay_sem.at[k]), -4, jnp.logical_and(z == 5, even))
    send_far(lambda k: (relay.at[part(k)], relay_sem.at[k]), -2, jnp.logical_and(z == 4, odd))
    send(images, ext.at[1], ext_sem.at[1], nextdoor[1], jnp.logical_and(odd, ~first))
    ready(2, even)
    send(texts, ext.at[0], ext_sem.at[0], nextdoor[0], even)
    for s in range(2):
        send_cross(s, jnp.logical_and(~cross_late, ~is_root(over[s])))

    def meet(pairs, positive=False):
        values = [block[...] for _, block in pairs]
        scores = [
            factor
            * lax.dot_general(
                own[side], value, (((1,), (1,)), ((), ())), preferred_element_type=jnp.float32
            )
            + offset
            for (side, _), value in zip(pairs, values)
        ]
        coefs, terms = [], []
        for score in scores:
            if positive:
                diagonal = lax.broadcasted_iota(jnp.int32, score.shape, 0) == lax.broadcasted_iota(
                    jnp.int32, score.shape, 1
                )
                score = jnp.where(diagonal, -score, score)
            small = jnp.exp(-jnp.abs(score))
            share = 1.0 / (1.0 + small)
            coef = jnp.where(score >= 0, share, small * share)
            if positive:
                coef = jnp.where(diagonal, -coef, coef)
            term = jnp.maximum(score, 0.0) + jnp.log1p(small)
            if score.shape[1] > rows:
                term = term[:, :rows] + term[:, rows:]
            coefs.append(coef.astype(jnp.bfloat16))
            terms.append(term)
        grads = [
            jnp.dot(coef, value, preferred_element_type=jnp.float32)
            for coef, value in zip(coefs, values)
        ]
        for (side, _), term, grad in zip(pairs, terms, grads):
            if positive:
                lacc[side] = term
                acc[side] = grad
            else:
                lacc[side] += term
                acc[side] += grad

    for load in loads:
        load.wait()
    factor, offset = scale[0], bias[0]
    meet([(side, own.at[1 - side]) for side in range(2)], positive=True)

    def meet_cross(when):
        @pl.when(when)
        def _():
            for s in range(2):
                arrived(cross.at[s], cross_sem.at[s])
            early = 1 - c
            arrived(ext.at[early], ext_sem.at[early])
            meet([(0, cross.at[0]), (1, cross.at[1]), (early, ext.at[early])])

    ready(2, odd)
    ready(1, late)
    send_own(1, late)
    ready(3, g >= 0)
    send(images, ext.at[1], ext_sem.at[1], nextdoor[1], jnp.logical_and(odd, first))
    for s in range(2):
        send_cross(s, jnp.logical_and(~cross_late, is_root(over[s])))

    by_root = jnp.logical_and(b < 16, g == 0)
    code = jnp.where(
        first,
        jnp.where(even, 19, 35),
        jnp.where(last, 19, jnp.where(z == 1, jnp.where(even, 14, 38), jnp.where(even, 26, 42))),
    )
    code = jnp.where(
        jnp.logical_and(by_root, z == 1),
        19,
        jnp.where(jnp.logical_and(by_root, z == 2), 22, jnp.where(jnp.logical_and(by_root, z == 3), 26, code)),
    )

    def stream_hop(i):
        s = lax.rem(code // (1 << i), 2)
        ups = sum(lax.rem(code // (1 << j), 2) for j in range(i)) if i else 0
        return s, jnp.where(s == 1, ups, i - ups)

    steps = [stream_hop(i) for i in range(2 * HOPS)]

    def stays(s):
        return jnp.logical_or(inner_up, s == 1)

    def ends(s):
        return jnp.logical_or(inner_down, s == 0)

    def pass_relay(when):
        for k in range(CHUNKS):
            here = relay.at[part(k)]
            relays = jnp.logical_and(when, jnp.logical_or(z == 3, even))

            @pl.when(relays)
            def _():
                arrived(here, relay_sem.at[k])

            send(here, lane(0, 2, k, c), hop_sem.at[0, 2, k], at(10), jnp.logical_and(jnp.logical_and(when, z == 3), even))
            send(here, ext.at[0, part(k)], late_sem(ext_sem, 0, k), at(9), jnp.logical_and(jnp.logical_and(when, z == 3), odd))
            send(here, ext.at[1, part(k)], late_sem(ext_sem, 1, k), at(-9), jnp.logical_and(jnp.logical_and(when, z == 4), even))

    def stage(i, k):
        mix = None
        if mix is None:
            return (*steps[i], k)
        base = i - i % 2
        j = (i - base) * CHUNKS + k
        (s0, h0), (s1, h1) = steps[base], steps[base + 1]
        pick = jnp.where(mix, j % 2, i - base)
        return (
            jnp.where(pick == 0, s0, s1),
            jnp.where(pick == 0, h0, h1),
            jnp.where(mix, j // 2, k),
        )

    def forwards(i, k):
        n = i * CHUNKS + k
        s, hop, k = stage(i, k)
        here = lane(s, hop, k, c)
        further = lane(s, lax.rem(hop + 1, HOPS), k, c)
        return (
            (
                copy_to(here, further, hop_sem.at[s, lax.rem(hop + 1, HOPS), k], at(2 - 4 * s), hop_send.at[n, 0]),
                jnp.logical_and(hop + 1 < HOPS, stays(s)),
            ),
            (
                copy_to(here, ext.at[s, part(k)], late_sem(ext_sem, s, k), at(1 - 2 * s), hop_send.at[n, 0]),
                jnp.logical_and(
                    jnp.logical_and(hop + 1 == HOPS, c == 1 - s), jnp.logical_and(stays(s), ends(s))
                ),
            ),
            (copy_to(here, here, sib_sem.at[s, hop, k], sib, hop_send.at[n, 1]), g >= 0),
        )

    for i in range(2 * HOPS + 1):
        if i < 2 * HOPS:
            for k in range(CHUNKS):
                s, hop, p = stage(i, k)
                arrived(lane(s, hop, p, c), hop_sem.at[s, hop, p])
                if i == 0 and k == 0:
                    send_far(lambda k: (lane(0, 1, k, c), hop_sem.at[0, 1, k]), 4, z == 6)
                for copy, when in forwards(i, k):
                    pl.when(when)(copy.start)
        if i == RELAY_AT:
            send_far(
                lambda k: (relay.at[part(k)], relay_sem.at[k]), 2, jnp.logical_and(z == 3, even), images
            )
            far_ready()
            pass_relay(z == 3)
        if i == RELAY_AT + 2:
            pass_relay(z == 4)
        if i == CROSS_AT:
            for s in range(2):
                send_cross(s, cross_late)
        if i == 3:
            meet_cross(jnp.logical_and(~cross_late, inner_down))
        if i in (2, 4, 6):
            for s, hop in steps[i - 2 : i]:
                for k in range(CHUNKS):
                    arrived(lane(s, hop, k, 1 - c), sib_sem.at[s, hop, k])
            meet([(s, pair.at[s, hop]) for s, hop in steps[i - 2 : i]])
    meet_cross(jnp.logical_or(first, cross_late))
    for k in range(CHUNKS):
        arrived(ext.at[c, part(k)], late_sem(ext_sem, c, k))
    meet([(c, ext.at[c])])

    for side in range(2):
        grad_out[side] = factor * acc[side]
    loss_out[...] = jnp.sum(lacc[0].T, axis=0, keepdims=True)
    for copy, when in sent:
        pl.when(when)(copy.wait_send)
    for i in range(2 * HOPS):
        for k in range(CHUNKS):
            for copy, when in forwards(i, k):
                pl.when(when)(copy.wait_send)


def late_sem(ext_sem, s, k):
    return ext_sem.at[2 + 2 * k + s]


def hand_over(loss_in, grad_in, loss_out, gimg_out, gtxt_out, sem):
    half = gimg_out.shape[0] // 2
    copies = [pltpu.make_async_copy(loss_in, loss_out, sem.at[4])]
    for side, out in enumerate((gimg_out, gtxt_out)):
        for k in range(2):
            rows = pl.ds(k * half, half)
            copies.append(
                pltpu.make_async_copy(grad_in.at[side, rows], out.at[rows], sem.at[2 * side + k])
            )
    for copy in copies:
        copy.start()
    for copy in copies:
        copy.wait()


def solution(mesh):
    n_blk, n_grp = mesh.shape["blk"], mesh.shape["grp"]

    def on_device(images, texts, scale, bias):
        rows, width = images.shape
        bf16, f32 = jnp.bfloat16, jnp.float32
        hbm = pl.BlockSpec(memory_space=pltpu.HBM)
        vmem = pl.BlockSpec(memory_space=pltpu.VMEM)
        anywhere = pl.BlockSpec(memory_space=pl.ANY)
        loss, grads = pl.pallas_call(
            functools.partial(kernel, n_blk, n_grp),
            out_shape=(
                jax.ShapeDtypeStruct((1, rows), f32),
                jax.ShapeDtypeStruct((2, rows, width), f32),
            ),
            in_specs=[vmem, hbm, hbm],
            out_specs=(vmem, vmem),
            scratch_shapes=[
                pltpu.VMEM((2, HOPS, 2 * rows, width), bf16),
                pltpu.VMEM((2, rows, width), bf16),
                pltpu.VMEM((2, rows, width), bf16),
                pltpu.VMEM((2, rows, width), f32),
                pltpu.VMEM((2, rows, rows), f32),
                pltpu.SemaphoreType.DMA((2,)),
                pltpu.VMEM((rows, width), bf16),
                pltpu.SemaphoreType.DMA((CHUNKS,)),
                pltpu.SemaphoreType.DMA((14 * CHUNKS + 9,)),
                pltpu.SemaphoreType.DMA((2 * HOPS * CHUNKS, 2)),
                pltpu.SemaphoreType.DMA((2, HOPS, CHUNKS)),
                pltpu.SemaphoreType.DMA((2, HOPS, CHUNKS)),
                pltpu.SemaphoreType.DMA((2 + 2 * CHUNKS,)),
                pltpu.SemaphoreType.DMA((2,)),
                pltpu.SemaphoreType.REGULAR((7,)),
                pltpu.SMEM((1,), f32),
                pltpu.SMEM((1,), f32),
            ],
            compiler_params=pltpu.CompilerParams(
                collective_id=0, has_side_effects=True, vmem_limit_bytes=VMEM_LIMIT
            ),
        )(jnp.stack((images, texts)), scale, bias)
        loss, gimg, gtxt = pl.pallas_call(
            hand_over,
            out_shape=(
                jax.ShapeDtypeStruct((1, rows), f32),
                jax.ShapeDtypeStruct((rows, width), f32),
                jax.ShapeDtypeStruct((rows, width), f32),
            ),
            in_specs=[anywhere] * 2,
            out_specs=(anywhere,) * 3,
            scratch_shapes=[pltpu.SemaphoreType.DMA((5,))],
            compiler_params=pltpu.CompilerParams(vmem_limit_bytes=VMEM_LIMIT),
        )(loss, grads)
        return loss.reshape(rows), gimg, gtxt

    block = P(("blk", "grp"), None)
    return jax.shard_map(
        on_device,
        mesh=mesh,
        in_specs=(block, block, P(), P()),
        out_specs=(P(("blk", "grp")), block, block),
        check_vma=False,
    )
```
